768 devices in a mesh: box: 192 (over y, z, core), grp: 4 (over x).
Axes of the slice: x: 4, y: 8, z: 12, core: 2. Of those that a mesh axis runs over, the one named last changes fastest.
Arguments:
- conserved_state: float32 [5, 1536, 32, 128], P(None, 'box', 'grp'), may hold values from -17 to 95, as said below
- box_source: int32 [384], replicated, may hold values from 0 to 383, as said below
Outputs:
- regridded: float32 [5, 1536, 32, 128], P(None, 'box', 'grp')
- potential: float32 [1536, 32, 128], P('box', 'grp')
The draws below stay inside these ranges and needn't reach their ends.
Inputs may be any that keep to these rules, and one draw needn't show every extreme that they name: `conserved_state`: the pressure of every cell is positive and so is its density. `box_source`: A permutation of the boxes. The box at position k comes from owner k // 2 or an owner next to it (no wrap); across each boundary between owners at most 1 boxes move in each direction, and exactly 1 in both directions across some boundary.
All inputs are finite; a program needn't handle non-finite values.
Results may differ from the reference program's by a relative error of at most 0.0003.
Values sent between devices are 32-bit elements; how exact they have to be, the bound alone decides.
No kernel may reach another device: no remote copies, remote signals or barrier semaphores. Data moves between devices by JAX's collectives and lax.ppermute only.
A program may use at most 32 MiB of HBM per device.

```python
import jax
import jax.numpy as jnp
from jax import lax

BX = 4
SLOTS = 2
MOVE = 1
PRE = 2
COARSE = 4
POST = 2
NX = 1536
NY = 32
NZ = 128
NBOXES = 384
N_BOX = 192


def draw_conserved_state(key, part):
    key = jax.random.fold_in(key, 11)
    subkeys = jax.random.split(key, 3)
    grid_shape = (NX, NY, NZ)
    ramp_scale = 1.0 + 2.0 * jnp.arange(NX, dtype=jnp.float32)[:, None, None] / NX
    density = ramp_scale * jax.random.uniform(subkeys[0], grid_shape, jnp.float32, 0.5, 1.5)
    velocity = ramp_scale * jnp.clip(0.4 * jax.random.normal(subkeys[1], (3,) + grid_shape, jnp.float32), -1.2, 1.2)
    pressure = jnp.exp(jax.random.uniform(subkeys[2], grid_shape, jnp.float32, -1.2, 1.2))
    energy = pressure * 1.5 + 0.5 * density * jnp.sum(velocity * velocity, axis=0)
    return jnp.concatenate([density[None], density[None] * velocity, energy[None]], axis=0)


def draw_box_source(key, part):
    key = jax.random.fold_in(key, 7)
    subkeys = jax.random.split(key, 3)
    owners = NBOXES // SLOTS
    owner_index = jnp.arange(owners, dtype=jnp.int32)
    moves = jax.random.randint(subkeys[0], (owners,), 0, MOVE + 1)
    chosen = jax.random.randint(subkeys[1], (), 0, owners - 1)
    moves = jnp.where(owner_index == chosen, MOVE, moves)
    moves = jnp.where(owner_index == owners - 1, 0, moves).astype(jnp.int32)
    left_moves = jnp.concatenate([jnp.zeros((1,), jnp.int32), moves[:-1]])
    slot_index = jnp.arange(SLOTS, dtype=jnp.int32)[None, :]
    base = owner_index[:, None] * SLOTS
    from_left = base - left_moves[:, None] + slot_index
    from_right = base + SLOTS + slot_index - (SLOTS - moves[:, None])
    sources = jnp.where(slot_index < left_moves[:, None], from_left, jnp.where(slot_index >= SLOTS - moves[:, None], from_right, base + slot_index))
    scores = jax.random.randint(subkeys[2], (owners, SLOTS), 0, 1 << 20) * SLOTS + slot_index
    ordering = jnp.argsort(scores, axis=1)
    sources = jnp.take_along_axis(sources, ordering, axis=1)
    return sources.reshape(-1).astype(jnp.int32)


def setup_inputs(seed: int = 0) -> dict:
    seeds = jax.random.split(jax.random.key(seed), 3)
    return {
        "conserved_state": draw_conserved_state(jax.random.fold_in(seeds[2], 71), 0),
        "box_source": draw_box_source(jax.random.fold_in(seeds[2], 71), 0),
    }


GAMMA = 5.0 / 3.0
COURANT = 0.3
OMEGA = 2.0 / 3.0
FOUR_PI_G = 2.0

def minmod(left_diff, right_diff):
    return 0.5 * (jnp.sign(left_diff) + jnp.sign(right_diff)) * jnp.minimum(jnp.abs(left_diff), jnp.abs(right_diff))

def primitive(conserved):
    density = conserved[0]
    velocity = conserved[1:4] / density
    kinetic = 0.5 * lax.optimization_barrier(jnp.sum(conserved[1:4] * velocity, axis=0))
    pressure = (GAMMA - 1.0) * (conserved[4] - kinetic)
    return jnp.concatenate([density[None], velocity, pressure[None]], axis=0)

def signal_speed(conserved):
    prim_state = primitive(conserved)
    sound_speed = jnp.sqrt(GAMMA * prim_state[4] / prim_state[0])
    return lax.optimization_barrier(jnp.max(jnp.abs(prim_state[1:4]), axis=0)) + sound_speed

def side_terms(face_state, normal):
    density = face_state[0]
    velocity = face_state[1:4]
    pressure = face_state[4]
    normal_speed = velocity[normal]
    energy = pressure / (GAMMA - 1.0) + 0.5 * density * lax.optimization_barrier(jnp.sum(velocity * velocity, axis=0))
    conserved = jnp.concatenate([density[None], density[None] * velocity, energy[None]], axis=0)
    momentum_flux = [density * normal_speed * velocity[component] + pressure * (1.0 if component == normal else 0.0) for component in range(3)]
    flux_terms = jnp.stack([density * normal_speed] + momentum_flux + [normal_speed * (energy + pressure)], axis=0)
    sound_speed = jnp.sqrt(GAMMA * pressure / density)
    return (conserved, flux_terms, normal_speed, sound_speed)

def hll_flux(left_state, right_state, normal):
    cons_left, flux_left, speed_left, sound_left = side_terms(left_state, normal)
    cons_right, flux_right, speed_right, sound_right = side_terms(right_state, normal)
    lowest = jnp.minimum(jnp.minimum(speed_left - sound_left, speed_right - sound_right), 0.0)
    highest = jnp.maximum(jnp.maximum(speed_left + sound_left, speed_right + sound_right), 0.0)
    return (highest * flux_left - lowest * flux_right + highest * lowest * (cons_right - cons_left)) / (highest - lowest)

def flux_balance(slab_cells, normal):
    axis_number = normal + 1
    length = slab_cells.shape[axis_number] - 4
    prim_state = primitive(slab_cells)
    differences = lax.slice_in_dim(prim_state, 1, length + 4, axis=axis_number) - lax.slice_in_dim(prim_state, 0, length + 3, axis=axis_number)
    slopes = minmod(lax.slice_in_dim(differences, 0, length + 2, axis=axis_number), lax.slice_in_dim(differences, 1, length + 3, axis=axis_number))
    left_state = lax.slice_in_dim(prim_state, 1, length + 2, axis=axis_number) + 0.5 * lax.slice_in_dim(slopes, 0, length + 1, axis=axis_number)
    right_state = lax.slice_in_dim(prim_state, 2, length + 3, axis=axis_number) - 0.5 * lax.slice_in_dim(slopes, 1, length + 2, axis=axis_number)
    fluxes = hll_flux(left_state, right_state, normal)
    return lax.slice_in_dim(fluxes, 1, length + 1, axis=axis_number) - lax.slice_in_dim(fluxes, 0, length, axis=axis_number)

def advance(padded, time_step):
    fields = padded[:5]
    potential = padded[5]
    interior = fields[:, 2:-2, 2:-2, 2:-2]
    balance = flux_balance(fields[:, :, 2:-2, 2:-2], 0)
    balance = balance + flux_balance(fields[:, 2:-2, :, 2:-2], 1)
    balance = balance + flux_balance(fields[:, 2:-2, 2:-2, :], 2)
    pull_first = 0.5 * (potential[1:-3, 2:-2, 2:-2] - potential[3:-1, 2:-2, 2:-2])
    pull_second = 0.5 * (potential[2:-2, 1:-3, 2:-2] - potential[2:-2, 3:-1, 2:-2])
    pull_third = 0.5 * (potential[2:-2, 2:-2, 1:-3] - potential[2:-2, 2:-2, 3:-1])
    gravity = jnp.stack([pull_first, pull_second, pull_third], axis=0)
    gained = jnp.concatenate([jnp.zeros_like(interior[:1]), interior[0][None] * gravity, lax.optimization_barrier(jnp.sum(interior[1:4] * gravity, axis=0))[None]], axis=0)
    return interior - time_step * balance + time_step * gained

def operator(padded):
    center = padded[1:-1, 1:-1, 1:-1]
    beside = padded[2:, 1:-1, 1:-1] + padded[:-2, 1:-1, 1:-1]
    beside = beside + padded[1:-1, 2:, 1:-1] + padded[1:-1, :-2, 1:-1]
    beside = beside + padded[1:-1, 1:-1, 2:] + padded[1:-1, 1:-1, :-2]
    return 6.0 * center - beside

def jacobi(grid_field, source):
    return grid_field + OMEGA / 6.0 * (source - operator(jnp.pad(grid_field, 1, mode='wrap')))

def restrict(grid_field):
    size_x, size_y, size_z = grid_field.shape
    grouped = grid_field.reshape(size_x // 2, 2, size_y // 2, 2, size_z // 2, 2)
    return 0.5 * lax.optimization_barrier(jnp.sum(grouped, axis=(1, 3, 5)))

def prolong(grid_field):
    return jnp.repeat(jnp.repeat(jnp.repeat(grid_field, 2, axis=0), 2, axis=1), 2, axis=2)

def reference(conserved_state, box_source):
    density = conserved_state[0]
    mean_density = jnp.sum(density) / (NX * NY * NZ)
    source = FOUR_PI_G * (mean_density - density)
    potential = OMEGA / 6.0 * source
    for number in range(PRE - 1):
        potential = jacobi(potential, source)
    residue = source - operator(jnp.pad(potential, 1, mode='wrap'))
    coarse_source = restrict(residue)
    correction = OMEGA / 6.0 * coarse_source
    for number in range(COARSE - 1):
        correction = jacobi(correction, coarse_source)
    potential = potential + prolong(correction)
    for number in range(POST):
        potential = jacobi(potential, source)
    time_step = COURANT / jnp.max(signal_speed(conserved_state))
    stacked = jnp.concatenate([conserved_state, potential[None]], axis=0)
    padded = jnp.pad(stacked, ((0, 0), (2, 2), (2, 2), (2, 2)), mode='wrap')
    block_rows = SLOTS * BX

    def one_block(number):
        piece = lax.dynamic_slice_in_dim(padded, number * block_rows, block_rows + 4, axis=1)
        return advance(piece, time_step)
    blocks = lax.map(one_block, jnp.arange(N_BOX, dtype=jnp.int32))
    updated = jnp.moveaxis(blocks, 0, 1).reshape(5, NX, NY, NZ)
    box_data = updated.reshape(5, NBOXES, BX, NY, NZ)
    regridded = jnp.take(box_data, box_source, axis=1).reshape(5, NX, NY, NZ)
    return (regridded, potential)
```

```python
import jax
import jax.numpy as jnp
from jax import lax
from jax.experimental import pallas as pl
from jax.experimental.pallas import tpu as pltpu
from jax.sharding import Mesh, PartitionSpec as P

GAMMA = 5.0 / 3.0
COURANT = 0.3
W = (2.0 / 3.0) / 6.0
BOX = ("y", "z", "c")
F32 = jnp.float32
CONST_GAIN = 40.0 / 9.0


def roll(value, shift, axis):
    return pltpu.roll(value, shift % value.shape[axis], axis)


def prim_of(rho, mx, my, mz, energy):
    inv = 1.0 / rho
    vx, vy, vz = mx * inv, my * inv, mz * inv
    kinetic = 0.5 * (mx * vx + my * vy + mz * vz)
    return rho, vx, vy, vz, (GAMMA - 1.0) * (energy - kinetic)


def half_slope(back, ahead):
    low = jnp.minimum(back, ahead)
    high = jnp.maximum(back, ahead)
    return 0.5 * (jnp.maximum(low, 0.0) + jnp.minimum(high, 0.0))


def side(state, normal):
    rho, pressure = state[0], state[4]
    vel = state[1:4]
    u = vel[normal]
    mom = [rho * v for v in vel]
    energy = pressure * 1.5 + 0.5 * (mom[0] * vel[0] + mom[1] * vel[1] + mom[2] * vel[2])
    flux = [mom[normal]] + [mom[normal] * v for v in vel] + [u * (energy + pressure)]
    flux[1 + normal] = flux[1 + normal] + pressure
    sound = jnp.sqrt(GAMMA * pressure / rho)
    return [rho] + mom + [energy], flux, u - sound, u + sound


def hll(left, right, normal):
    cons_l, flux_l, slow_l, fast_l = side(left, normal)
    cons_r, flux_r, slow_r, fast_r = side(right, normal)
    low = jnp.minimum(jnp.minimum(slow_l, slow_r), 0.0)
    high = jnp.maximum(jnp.maximum(fast_l, fast_r), 0.0)
    inv = 1.0 / (high - low)
    a = high * inv
    b = low * inv
    ab = high * b
    return [a * fl - b * fr + ab * (cr - cl) for fl, fr, cl, cr in zip(flux_l, flux_r, cons_l, cons_r)]


def pack_rows_kernel(ids, cs, out, loc):
    g = ids[1]
    count = out.shape[0]
    row = lax.broadcasted_iota(jnp.int32, (8, 128), 0)
    mass = jnp.zeros((8, 128), F32)
    speed = jnp.zeros((8, 128), F32)
    for p in range(8):
        vals = [cs[f, p] for f in range(5)]
        rho, vx, vy, vz, pressure = prim_of(*vals)
        top = jnp.maximum(jnp.maximum(jnp.abs(vx), jnp.abs(vy)), jnp.abs(vz))
        speed = jnp.maximum(speed, top + jnp.sqrt(GAMMA * pressure / rho))
        mass = mass + rho
        last = jnp.zeros((8, 128), F32)
        first = jnp.zeros((8, 128), F32)
        for k in range(4):
            mine = (row // 2) == k
            last = jnp.where(mine, roll(vals[k + 1], 2 * k - 6, 0), last)
            first = jnp.where(mine, roll(vals[k + 1], 2 * k, 0), first)
        for j in range(count):
            out[j, p] = vals[0]
            out[j, 8 + p] = jnp.where(lax.rem(j - g + count, count) == 1, last, first)
    tile = jnp.where(row < 4, jnp.sum(mass), jnp.max(speed))
    loc[...] = tile
    for j in range(count):
        out[j, 16] = tile


def pack_planes_kernel(ids, cs, rows, up1, dn1, up2, dn2, red):
    g = ids[1]
    count = rows.shape[0]
    for t in range(4):
        src = lax.rem(g + t, count)
        for p in range(8):
            tile = rows[src, p]
            up1[4 * p + t] = tile
            dn1[4 * p + t] = tile
            if p >= 4:
                up2[4 * (p - 4) + t] = tile
            else:
                dn2[4 * p + t] = tile
    for f in range(4):
        for p in range(2):
            up1[32 + 2 * f + p] = cs[f + 1, 6 + p]
            dn1[32 + 2 * f + p] = cs[f + 1, p]
    mass = rows[0, 16][0:1]
    speed = rows[0, 16][4:5]
    for j in range(1, count):
        mass = mass + rows[j, 16][0:1]
        speed = jnp.maximum(speed, rows[j, 16][4:5])
    lane = lax.broadcasted_iota(jnp.int32, (1, 128), 1)
    line = jnp.where(lane < 64, mass, speed)
    for j in range(red.shape[0]):
        red[j] = line


def fold_kernel(got, out):
    mass = got[0]
    speed = got[0]
    for j in range(1, got.shape[0]):
        mass = mass + got[j]
        speed = jnp.maximum(speed, got[j])
    lane = lax.broadcasted_iota(jnp.int32, (1, 128), 1)
    line = jnp.where(lane < 64, mass, speed)
    for j in range(out.shape[0]):
        out[j] = line


def main_kernel(ids, boxes, loc, cs, rows, up1, dn1, up2, dn2, phi_out, delta, send_up, send_dn,
                src, fine, coarse_src, coarse_a, coarse_b, grav, prims, halo):
    b, g = ids[0], ids[1]
    count = rows.shape[0]
    rho_loc = loc[0:1, :] * (1.0 / 8192.0)

    for t in range(4):
        own = lax.rem(g + t, count)
        at = pl.ds(8 * t, 8)
        for p in range(4):
            src[p, at, :] = 2.0 * (rho_loc - up2[4 * p + t])
            src[28 + p, at, :] = 2.0 * (rho_loc - dn2[4 * p + t])
        for p in range(8):
            src[4 + p, at, :] = 2.0 * (rho_loc - up1[4 * p + t])
            src[12 + p, at, :] = 2.0 * (rho_loc - rows[own, p])
            src[20 + p, at, :] = 2.0 * (rho_loc - dn1[4 * p + t])

    def beside(below, here, above, step):
        total = below + above
        total = total + (roll(here, step, 0) + roll(here, -step, 0))
        return total + (roll(here, step, 1) + roll(here, -step, 1))

    head = 2.0 * W - 6.0 * W * W
    for p in range(1, 31):
        s = src[p]
        fine[p] = head * s + (W * W) * beside(src[p - 1], s, src[p + 1], 1)

    def residue(p):
        v = fine[p]
        return src[p] - 6.0 * v + beside(fine[p - 1], v, fine[p + 1], 1)

    even_y = lax.broadcasted_iota(jnp.int32, (32, 128), 0) % 2 == 0
    even_z = lax.broadcasted_iota(jnp.int32, (32, 128), 1) % 2 == 0
    for c in range(14):
        r = residue(2 + 2 * c) + residue(3 + 2 * c)
        r = r + jnp.where(even_y, roll(r, -1, 0), roll(r, 1, 0))
        r = r + jnp.where(even_z, roll(r, -1, 1), roll(r, 1, 1))
        coarse_src[c] = 0.5 * r
    for c in range(1, 13):
        s = coarse_src[c]
        coarse_a[c] = head * s + (W * W) * beside(coarse_src[c - 1], s, coarse_src[c + 1], 2)

    def relax(ref, right, n, step):
        v = ref[n]
        return (1.0 / 3.0) * v + W * (right + beside(ref[n - 1], v, ref[n + 1], step))

    for c in range(2, 12):
        coarse_b[c] = relax(coarse_a, coarse_src[c], c, 2)
    for c in range(3, 11):
        corr = relax(coarse_b, coarse_src[c], c, 2)
        for p in (2 * c + 2, 2 * c + 3):
            if 9 <= p <= 22:
                fine[p] = fine[p] + corr
    for p in range(10, 22):
        coarse_a[p - 9] = relax(fine, src[p], p, 1)
    for p in range(11, 21):
        coarse_b[p - 10] = relax(coarse_a, src[p], p - 9, 1)
    for p in range(8):
        v = coarse_b[p + 2]
        phi_out[p] = v[0:8]
        grav[0, p] = 0.5 * (coarse_b[p + 1, 0:8, :] - coarse_b[p + 3, 0:8, :])
        grav[1, p] = 0.5 * (roll(v, 1, 0) - roll(v, -1, 0))[0:8]
        own_rows = v[0:8]
        grav[2, p] = 0.5 * (roll(own_rows, 1, 1) - roll(own_rows, -1, 1))

    def put(ref, n, vals):
        for f, v in enumerate(prim_of(*vals)):
            ref[f, n] = v

    for p in range(2):
        put(prims, p, [up1[4 * (6 + p)]] + [up1[32 + 2 * f + p] for f in range(4)])
        put(prims, 10 + p, [dn1[4 * p]] + [dn1[32 + 2 * f + p] for f in range(4)])
    row = lax.broadcasted_iota(jnp.int32, (8, 128), 0)
    nxt = lax.rem(g + 1, count)
    prv = lax.rem(g + count - 1, count)
    for p in range(8):
        put(prims, 2 + p, [cs[f, p] for f in range(5)])
        ahead, behind = rows[nxt, 8 + p], rows[prv, 8 + p]
        vals = [jnp.where(row < 4, rows[nxt, p], rows[prv, p])]
        for k in range(4):
            vals.append(jnp.where(row < 4, roll(ahead, -2 * k, 0), roll(behind, 6 - 2 * k, 0)))
        put(halo, p, vals)

    def face_x(n):
        states = []
        for m, sign in ((n, 1.0), (n + 1, -1.0)):
            out = []
            for f in range(5):
                mid = prims[f, m]
                out.append(mid + sign * half_slope(mid - prims[f, m - 1], prims[f, m + 1] - mid))
            states.append(out)
        return hll(states[0], states[1], 0)

    def roll_faces(vals, normal, axis):
        left, right = [], []
        for v in vals:
            diff = roll(v, -1, axis) - v
            slope = half_slope(roll(diff, 1, axis), diff)
            left.append(v + slope)
            right.append(roll(v - slope, -1, axis))
        flux = hll(left, right, normal)
        return [fl - roll(fl, 1, axis) for fl in flux]

    def plane(p, before):
        after = face_x(p + 2)
        balance = [x - y for x, y in zip(after, before)]
        here = [prims[f, p + 2] for f in range(5)]
        tall = [jnp.concatenate([here[f], halo[f, p]], axis=0) for f in range(5)]
        for f, v in enumerate(roll_faces(tall, 1, 0)):
            balance[f] = balance[f] + v[0:8]
        for f, v in enumerate(roll_faces(here, 2, 1)):
            balance[f] = balance[f] + v
        pulls = [grav[d, p] for d in range(3)]
        moms = [cs[d + 1, p] for d in range(3)]
        delta[0, p] = -balance[0]
        for d in range(3):
            delta[d + 1, p] = cs[0, p] * pulls[d] - balance[d + 1]
        delta[4, p] = (moms[0] * pulls[0] + moms[1] * pulls[1] + moms[2] * pulls[2]) - balance[4]
        return tuple(after)

    lax.fori_loop(0, 8, plane, tuple(face_x(1)))

    last = boxes.shape[0] // 2 - 1
    for side_owner, send in ((jnp.minimum(b + 1, last), send_up), (jnp.maximum(b - 1, 0), send_dn)):
        second = jnp.logical_or(boxes[2 * side_owner] == 2 * b + 1, boxes[2 * side_owner + 1] == 2 * b + 1)
        start = jnp.where(second, 4, 0)
        for f in range(5):
            for p in range(4):
                send[f, p] = cs[f, start + p]
                send[5 + f, p] = delta[f, start + p]


def final_kernel(ids, boxes, loc, got, cs, delta, phi, from_dn, from_up, out, potential, *, cells):
    b = ids[0]
    mass = got[0]
    speed = got[0]
    for j in range(1, got.shape[0]):
        mass = mass + got[j]
        speed = jnp.maximum(speed, got[j])
    mass = jnp.broadcast_to(mass[:, 0:1], (1, 128))
    speed = jnp.broadcast_to(speed[:, 64:65], (1, 128))
    shift = CONST_GAIN * (mass / cells - loc[0:1, :] * (1.0 / 8192.0))
    step = COURANT / speed
    for p in range(8):
        potential[p] = phi[p] + shift
    for slot in range(2):
        rel = boxes[2 * b + slot] - 2 * b

        @pl.when(rel < 0)
        def _():
            for f in range(5):
                for p in range(4):
                    out[f, 4 * slot + p] = from_dn[f, p] + step * from_dn[5 + f, p]

        @pl.when(rel > 1)
        def _():
            for f in range(5):
                for p in range(4):
                    out[f, 4 * slot + p] = from_up[f, p] + step * from_up[5 + f, p]

        @pl.when(jnp.logical_and(rel >= 0, rel <= 1))
        def _():
            start = 4 * jnp.clip(rel, 0, 1)
            for f in range(5):
                for p in range(4):
                    out[f, 4 * slot + p] = cs[f, start + p] + step * delta[f, start + p]


def call(kernel, outs, scalars, scratch, *args):
    shapes = [jax.ShapeDtypeStruct(s, F32) for s in outs]
    smem = pl.BlockSpec(memory_space=pltpu.SMEM)
    vmem = pl.BlockSpec(memory_space=pltpu.VMEM)
    return pl.pallas_call(
        kernel,
        out_shape=shapes,
        in_specs=[smem if i < scalars else vmem for i in range(len(args))],
        out_specs=[vmem] * len(outs),
        scratch_shapes=[pltpu.VMEM(s, F32) for s in scratch],
        compiler_params=pltpu.CompilerParams(vmem_limit_bytes=16 * 1024 * 1024),
    )(*args)


def shards(cs, boxes):
    ids = jnp.stack([lax.axis_index(BOX), lax.axis_index("x")]).astype(jnp.int32)
    n_box, n_grp = lax.axis_size(BOX), lax.axis_size("x")
    cells = float(cs[0].size * n_box * n_grp)

    def shift(value, by):
        return lax.ppermute(value, BOX, [(i, (i + by) % n_box) for i in range(n_box)])

    packed, loc = call(pack_rows_kernel, [(n_grp, 17, 8, 128), (8, 128)], 1, [], ids, cs)
    rows = lax.all_to_all(packed, "x", 0, 0, tiled=True)
    n_zc = lax.axis_size(("z", "c"))
    n_y = lax.axis_size("y")
    up1, dn1, up2, dn2, red = call(
        pack_planes_kernel,
        [(40, 8, 128), (40, 8, 128), (16, 8, 128), (16, 8, 128), (n_zc, 1, 128)],
        1, [], ids, cs, rows)
    up1, dn1, up2, dn2 = shift(up1, 1), shift(dn1, -1), shift(up2, 2), shift(dn2, -2)
    red = lax.all_to_all(red, ("z", "c"), 0, 0, tiled=True)
    red, boxes_late = lax.optimization_barrier((red, boxes))
    (red,) = call(fold_kernel, [(n_y, 1, 128)], 0, [], red)
    red = lax.all_to_all(red, "y", 0, 0, tiled=True)
    state = (5, 8, 8, 128)
    phi, delta, send_up, send_dn = call(
        main_kernel,
        [(8, 8, 128), state, (10, 4, 8, 128), (10, 4, 8, 128)],
        2,
        [(32, 32, 128), (32, 32, 128), (14, 32, 128), (14, 32, 128), (14, 32, 128),
         (3, 8, 8, 128), (5, 12, 8, 128), state],
        ids, boxes_late, loc, cs, rows, up1, dn1, up2, dn2)
    from_dn, from_up = shift(send_up, 1), shift(send_dn, -1)

    def last(*refs):
        final_kernel(*refs, cells=cells)

    return call(last, [state, (8, 8, 128)], 2, [], ids, boxes, loc, red, cs, delta, phi, from_dn, from_up)


def solution(mesh):
    n_box, n_grp = mesh.devices.shape
    parts = (8, n_box // 16, 2) if n_box % 16 == 0 else (2, n_box // 4, 2)
    fine_mesh = Mesh(mesh.devices.reshape(*parts, n_grp), ("y", "z", "c", "x"))
    return jax.shard_map(
        lambda a, b: tuple(shards(a, b)),
        mesh=fine_mesh,
        in_specs=(P(None, BOX, "x", None), P()),
        out_specs=(P(None, BOX, "x", None), P(BOX, "x", None)),
        check_vma=False,
    )
```

```python
import jax
import jax.numpy as jnp
from jax import lax
from jax.experimental import pallas as pl
from jax.experimental.pallas import tpu as pltpu
from jax.sharding import Mesh, PartitionSpec as P

GAMMA = 5.0 / 3.0
COURANT = 0.3
W = (2.0 / 3.0) / 6.0
BOX = ("y", "z", "c")
F32 = jnp.float32
CONST_GAIN = 40.0 / 9.0


def roll(value, shift, axis):
    return pltpu.roll(value, shift % value.shape[axis], axis)


def prim_of(rho, mx, my, mz, energy):
    inv = 1.0 / rho
    vx, vy, vz = mx * inv, my * inv, mz * inv
    kinetic = 0.5 * (mx * vx + my * vy + mz * vz)
    return rho, vx, vy, vz, (GAMMA - 1.0) * (energy - kinetic)


def half_slope(back, ahead):
    low = jnp.minimum(back, ahead)
    high = jnp.maximum(back, ahead)
    return 0.5 * (jnp.maximum(low, 0.0) + jnp.minimum(high, 0.0))


def side(state, normal):
    rho, pressure = state[0], state[4]
    vel = state[1:4]
    u = vel[normal]
    mom = [rho * v for v in vel]
    energy = pressure * 1.5 + 0.5 * (mom[0] * vel[0] + mom[1] * vel[1] + mom[2] * vel[2])
    flux = [mom[normal]] + [mom[normal] * v for v in vel] + [u * (energy + pressure)]
    flux[1 + normal] = flux[1 + normal] + pressure
    sound = jnp.sqrt(GAMMA * pressure / rho)
    return [rho] + mom + [energy], flux, u - sound, u + sound


def hll(left, right, normal):
    cons_l, flux_l, slow_l, fast_l = side(left, normal)
    cons_r, flux_r, slow_r, fast_r = side(right, normal)
    low = jnp.minimum(jnp.minimum(slow_l, slow_r), 0.0)
    high = jnp.maximum(jnp.maximum(fast_l, fast_r), 0.0)
    inv = 1.0 / (high - low)
    a = high * inv
    b = low * inv
    ab = high * b
    return [a * fl - b * fr + ab * (cr - cl) for fl, fr, cl, cr in zip(flux_l, flux_r, cons_l, cons_r)]


def pack_rows_kernel(ids, chip, out, loc):
    b, g = ids[0], ids[1]
    core = lax.rem(b, 2)
    count = out.shape[0]
    row = lax.broadcasted_iota(jnp.int32, (8, 128), 0)
    mass = jnp.zeros((8, 128), F32)
    speed = jnp.zeros((8, 128), F32)
    for p in range(16):
        vals = [chip[p // 8, f, p % 8] for f in range(5)]
        rho, vx, vy, vz, pressure = prim_of(*vals)
        top = jnp.maximum(jnp.maximum(jnp.abs(vx), jnp.abs(vy)), jnp.abs(vz))
        speed = jnp.maximum(speed, top + jnp.sqrt(GAMMA * pressure / rho))
        mass = mass + rho
        for j in range(count):
            out[j, p] = rho
    for p in range(8):
        last = jnp.zeros((8, 128), F32)
        first = jnp.zeros((8, 128), F32)
        for k in range(4):
            mine = (row // 2) == k
            val = chip[core, k + 1, p]
            last = jnp.where(mine, roll(val, 2 * k - 6, 0), last)
            first = jnp.where(mine, roll(val, 2 * k, 0), first)
        for j in range(count):
            out[j, 16 + p] = jnp.where(lax.rem(j - g + count, count) == 1, last, first)
    tile = jnp.where(row < 4, jnp.sum(mass), jnp.max(speed))
    loc[...] = tile
    for j in range(count):
        out[j, 24] = tile


def pack_planes_kernel(ids, chip, rows, pair, red):
    b, g = ids[0], ids[1]
    core = lax.rem(b, 2)
    count = rows.shape[0]
    for t in range(4):
        src = lax.rem(g + t, count)
        for i in range(12):
            pair[4 * i + t] = rows[src, 4 * core + i]
    for f in range(4):
        for p in range(2):
            pair[48 + 2 * f + p] = chip[core, f + 1, 6 * core + p]
    mass = rows[0, 24][0:1]
    speed = rows[0, 24][4:5]
    for j in range(1, count):
        mass = mass + rows[j, 24][0:1]
        speed = jnp.maximum(speed, rows[j, 24][4:5])
    lane = lax.broadcasted_iota(jnp.int32, (1, 128), 1)
    line = jnp.where(lane < 64, mass, speed)
    for j in range(red.shape[0]):
        red[j] = line


def fold_kernel(got, out):
    mass = got[0]
    speed = got[0]
    for j in range(1, got.shape[0]):
        mass = mass + got[j]
        speed = jnp.maximum(speed, got[j])
    lane = lax.broadcasted_iota(jnp.int32, (1, 128), 1)
    line = jnp.where(lane < 64, mass, speed)
    for j in range(out.shape[0]):
        out[j] = line


def main_kernel(ids, boxes, loc, chip, rows, pairs, phi_out, delta, send,
                wide, fine, coarse_src, coarse_a, coarse_b, grav, prims, halo):
    b, g = ids[0], ids[1]
    core = lax.rem(b, 2)
    count = rows.shape[0]
    rho_loc = loc[0:1, :] * (1.0 / 16384.0)

    for t in range(4):
        own = lax.rem(g + t, count)
        at = pl.ds(8 * t, 8)
        for i in range(12):
            wide[i, at, :] = 2.0 * (rho_loc - pairs[0, 4 * i + t])
            wide[28 + i, at, :] = 2.0 * (rho_loc - pairs[1, 4 * i + t])
        for p in range(16):
            wide[12 + p, at, :] = 2.0 * (rho_loc - rows[own, p])
    src = wide.at[pl.ds(8 * core, 32)]

    def beside(below, here, above, step):
        total = below + above
        total = total + (roll(here, step, 0) + roll(here, -step, 0))
        return total + (roll(here, step, 1) + roll(here, -step, 1))

    head = 2.0 * W - 6.0 * W * W
    for p in range(1, 31):
        s = src[p]
        fine[p] = head * s + (W * W) * beside(src[p - 1], s, src[p + 1], 1)

    def residue(p):
        v = fine[p]
        return src[p] - 6.0 * v + beside(fine[p - 1], v, fine[p + 1], 1)

    even_y = lax.broadcasted_iota(jnp.int32, (32, 128), 0) % 2 == 0
    even_z = lax.broadcasted_iota(jnp.int32, (32, 128), 1) % 2 == 0
    for c in range(14):
        r = residue(2 + 2 * c) + residue(3 + 2 * c)
        r = r + jnp.where(even_y, roll(r, -1, 0), roll(r, 1, 0))
        r = r + jnp.where(even_z, roll(r, -1, 1), roll(r, 1, 1))
        coarse_src[c] = 0.5 * r
    for c in range(1, 13):
        s = coarse_src[c]
        coarse_a[c] = head * s + (W * W) * beside(coarse_src[c - 1], s, coarse_src[c + 1], 2)

    def relax(ref, right, n, step):
        v = ref[n]
        return (1.0 / 3.0) * v + W * (right + beside(ref[n - 1], v, ref[n + 1], step))

    for c in range(2, 12):
        coarse_b[c] = relax(coarse_a, coarse_src[c], c, 2)
    for c in range(3, 11):
        corr = relax(coarse_b, coarse_src[c], c, 2)
        for p in (2 * c + 2, 2 * c + 3):
            if 9 <= p <= 22:
                fine[p] = fine[p] + corr
    for p in range(10, 22):
        coarse_a[p - 9] = relax(fine, src[p], p, 1)
    for p in range(11, 21):
        coarse_b[p - 10] = relax(coarse_a, src[p], p - 9, 1)
    for p in range(8):
        v = coarse_b[p + 2]
        phi_out[p] = v[0:8]
        grav[0, p] = 0.5 * (coarse_b[p + 1, 0:8, :] - coarse_b[p + 3, 0:8, :])
        grav[1, p] = 0.5 * (roll(v, 1, 0) - roll(v, -1, 0))[0:8]
        own_rows = v[0:8]
        grav[2, p] = 0.5 * (roll(own_rows, 1, 1) - roll(own_rows, -1, 1))

    def put(ref, n, vals):
        for f, v in enumerate(prim_of(*vals)):
            ref[f, n] = v

    other = 1 - core
    for p in range(2):
        put(prims, 10 * core + p,
            [pairs[core, 40 * other + 4 * p]] + [pairs[core, 48 + 2 * f + p] for f in range(4)])
        put(prims, 10 * other + p, [chip[other, f, 6 * core + p] for f in range(5)])
    row = lax.broadcasted_iota(jnp.int32, (8, 128), 0)
    nxt = lax.rem(g + 1, count)
    prv = lax.rem(g + count - 1, count)
    for p in range(8):
        put(prims, 2 + p, [chip[core, f, p] for f in range(5)])
        ahead, behind = rows[nxt, 16 + p], rows[prv, 16 + p]
        at = 8 * core + p
        vals = [jnp.where(row < 4, rows[nxt, at], rows[prv, at])]
        for k in range(4):
            vals.append(jnp.where(row < 4, roll(ahead, -2 * k, 0), roll(behind, 6 - 2 * k, 0)))
        put(halo, p, vals)

    def face_x(n):
        states = []
        for m, sign in ((n, 1.0), (n + 1, -1.0)):
            out = []
            for f in range(5):
                mid = prims[f, m]
                out.append(mid + sign * half_slope(mid - prims[f, m - 1], prims[f, m + 1] - mid))
            states.append(out)
        return hll(states[0], states[1], 0)

    def roll_faces(vals, normal, axis):
        left, right = [], []
        for v in vals:
            diff = roll(v, -1, axis) - v
            slope = half_slope(roll(diff, 1, axis), diff)
            left.append(v + slope)
            right.append(roll(v - slope, -1, axis))
        flux = hll(left, right, normal)
        return [fl - roll(fl, 1, axis) for fl in flux]

    def plane(p, before):
        after = face_x(p + 2)
        balance = [x - y for x, y in zip(after, before)]
        here = [prims[f, p + 2] for f in range(5)]
        tall = [jnp.concatenate([here[f], halo[f, p]], axis=0) for f in range(5)]
        for f, v in enumerate(roll_faces(tall, 1, 0)):
            balance[f] = balance[f] + v[0:8]
        for f, v in enumerate(roll_faces(here, 2, 1)):
            balance[f] = balance[f] + v
        pulls = [grav[d, p] for d in range(3)]
        moms = [chip[core, d + 1, p] for d in range(3)]
        delta[0, p] = -balance[0]
        for d in range(3):
            delta[d + 1, p] = chip[core, 0, p] * pulls[d] - balance[d + 1]
        delta[4, p] = (moms[0] * pulls[0] + moms[1] * pulls[1] + moms[2] * pulls[2]) - balance[4]
        return tuple(after)

    lax.fori_loop(0, 8, plane, tuple(face_x(1)))

    last = boxes.shape[0] // 2 - 1
    owner = jnp.clip(b + 2 * core - 1, 0, last)
    second = jnp.logical_or(boxes[2 * owner] == 2 * b + 1, boxes[2 * owner + 1] == 2 * b + 1)
    start = jnp.where(second, 4, 0)
    for f in range(5):
        for p in range(4):
            send[f, p] = chip[core, f, start + p]
            send[5 + f, p] = delta[f, start + p]


def final_kernel(ids, boxes, loc, got, chip, deltas, phi, came, out, potential, *, cells):
    b = ids[0]
    core = lax.rem(b, 2)
    mass = got[0]
    speed = got[0]
    for j in range(1, got.shape[0]):
        mass = mass + got[j]
        speed = jnp.maximum(speed, got[j])
    mass = jnp.broadcast_to(mass[:, 0:1], (1, 128))
    speed = jnp.broadcast_to(speed[:, 64:65], (1, 128))
    shift = CONST_GAIN * (mass / cells - loc[0:1, :] * (1.0 / 16384.0))
    step = COURANT / speed
    for p in range(8):
        potential[p] = phi[p] + shift
    for slot in range(2):
        place = boxes[2 * b + slot] - 2 * (b - core)
        inside = jnp.logical_and(place >= 0, place <= 3)

        @pl.when(inside)
        def _():
            near = jnp.clip(place, 0, 3)
            half, start = near // 2, 4 * lax.rem(near, 2)
            for f in range(5):
                for p in range(4):
                    out[f, 4 * slot + p] = chip[half, f, start + p] + step * deltas[half, f, start + p]

        @pl.when(jnp.logical_not(inside))
        def _():
            for f in range(5):
                for p in range(4):
                    out[f, 4 * slot + p] = came[f, p] + step * came[5 + f, p]


def call(kernel, outs, scalars, scratch, *args):
    shapes = [jax.ShapeDtypeStruct(s, F32) for s in outs]
    smem = pl.BlockSpec(memory_space=pltpu.SMEM)
    vmem = pl.BlockSpec(memory_space=pltpu.VMEM)
    return pl.pallas_call(
        kernel,
        out_shape=shapes,
        in_specs=[smem if i < scalars else vmem for i in range(len(args))],
        out_specs=[vmem] * len(outs),
        scratch_shapes=[pltpu.VMEM(s, F32) for s in scratch],
        compiler_params=pltpu.CompilerParams(vmem_limit_bytes=16 * 1024 * 1024),
    )(*args)


def shards(cs, boxes):
    ids = jnp.stack([lax.axis_index(BOX), lax.axis_index("x")]).astype(jnp.int32)
    n_box, n_grp = lax.axis_size(BOX), lax.axis_size("x")
    n_z, n_y = lax.axis_size("z"), lax.axis_size("y")
    cells = float(cs[0].size * n_box * n_grp)
    mates = [(i, (i + 2 * (i % 2) - 1) % n_box) for i in range(n_box)]

    chip = lax.all_gather(cs, "c")
    packed, loc = call(pack_rows_kernel, [(n_grp, 25, 8, 128), (8, 128)], 1, [], ids, chip)
    rows = lax.all_to_all(packed, "x", 0, 0, tiled=True)
    pair, red = call(pack_planes_kernel, [(56, 8, 128), (n_z, 1, 128)], 1, [], ids, chip, rows)
    pair = lax.ppermute(pair, BOX, mates)
    red = lax.all_to_all(red, "z", 0, 0, tiled=True)
    red, pair = lax.optimization_barrier((red, pair))
    pairs = lax.all_gather(pair, "c")
    (red,) = call(fold_kernel, [(n_y, 1, 128)], 0, [], red)
    red = lax.all_to_all(red, "y", 0, 0, tiled=True)
    state = (5, 8, 8, 128)
    phi, delta, send = call(
        main_kernel,
        [(8, 8, 128), state, (10, 4, 8, 128)],
        2,
        [(40, 32, 128), (32, 32, 128), (14, 32, 128), (14, 32, 128), (14, 32, 128),
         (3, 8, 8, 128), (5, 12, 8, 128), state],
        ids, boxes, loc, chip, rows, pairs)
    came = lax.ppermute(send, BOX, mates)
    deltas = lax.all_gather(delta, "c")

    def last(*refs):
        final_kernel(*refs, cells=cells)

    return call(last, [state, (8, 8, 128)], 2, [], ids, boxes, loc, red, chip, deltas, phi, came)


def solution(mesh):
    n_box, n_grp = mesh.devices.shape
    parts = (8, n_box // 16, 2) if n_box % 16 == 0 else (2, n_box // 4, 2)
    fine_mesh = Mesh(mesh.devices.reshape(*parts, n_grp), ("y", "z", "c", "x"))
    return jax.shard_map(
        lambda a, b: tuple(shards(a, b)),
        mesh=fine_mesh,
        in_specs=(P(None, BOX, "x", None), P()),
        out_specs=(P(None, BOX, "x", None), P(BOX, "x", None)),
        check_vma=False,
    )
```

```python
import jax
import jax.numpy as jnp
from jax import lax
from jax.experimental import pallas as pl
from jax.experimental.pallas import tpu as pltpu
from jax.sharding import Mesh, PartitionSpec as P

GAMMA = 5.0 / 3.0
COURANT = 0.3
W = (2.0 / 3.0) / 6.0
BOX = ("y", "z", "c")
F32 = jnp.float32
CONST_GAIN = 40.0 / 9.0


def roll(value, shift, axis):
    return pltpu.roll(value, shift % value.shape[axis], axis)


def prim_of(rho, mx, my, mz, energy):
    inv = 1.0 / rho
    vx, vy, vz = mx * inv, my * inv, mz * inv
    kinetic = 0.5 * (mx * vx + my * vy + mz * vz)
    return rho, vx, vy, vz, (GAMMA - 1.0) * (energy - kinetic)


def half_slope(back, ahead):
    low = jnp.minimum(back, ahead)
    high = jnp.maximum(back, ahead)
    return 0.5 * (jnp.maximum(low, 0.0) + jnp.minimum(high, 0.0))


def side(state, normal):
    rho, pressure = state[0], state[4]
    vel = state[1:4]
    u = vel[normal]
    mom = [rho * v for v in vel]
    energy = pressure * 1.5 + 0.5 * (mom[0] * vel[0] + mom[1] * vel[1] + mom[2] * vel[2])
    flux = [mom[normal]] + [mom[normal] * v for v in vel] + [u * (energy + pressure)]
    flux[1 + normal] = flux[1 + normal] + pressure
    sound = jnp.sqrt(GAMMA * pressure / rho)
    return [rho] + mom + [energy], flux, u - sound, u + sound


def hll(left, right, normal):
    cons_l, flux_l, slow_l, fast_l = side(left, normal)
    cons_r, flux_r, slow_r, fast_r = side(right, normal)
    low = jnp.minimum(jnp.minimum(slow_l, slow_r), 0.0)
    high = jnp.maximum(jnp.maximum(fast_l, fast_r), 0.0)
    inv = 1.0 / (high - low)
    a = high * inv
    b = low * inv
    ab = high * b
    return [a * fl - b * fr + ab * (cr - cl) for fl, fr, cl, cr in zip(flux_l, flux_r, cons_l, cons_r)]


def pack_rows_kernel(ids, cs, out, loc):
    g = ids[1]
    count = out.shape[0]
    row = lax.broadcasted_iota(jnp.int32, (8, 128), 0)
    mass = jnp.zeros((8, 128), F32)
    speed = jnp.zeros((8, 128), F32)
    for p in range(8):
        vals = [cs[f, p] for f in range(5)]
        rho, vx, vy, vz, pressure = prim_of(*vals)
        top = jnp.maximum(jnp.maximum(jnp.abs(vx), jnp.abs(vy)), jnp.abs(vz))
        speed = jnp.maximum(speed, top + jnp.sqrt(GAMMA * pressure / rho))
        mass = mass + rho
        last = jnp.zeros((8, 128), F32)
        first = jnp.zeros((8, 128), F32)
        for k in range(4):
            mine = (row // 2) == k
            last = jnp.where(mine, roll(vals[k + 1], 2 * k - 6, 0), last)
            first = jnp.where(mine, roll(vals[k + 1], 2 * k, 0), first)
        for j in range(count):
            out[j, p] = rho
            out[j, 8 + p] = jnp.where(lax.rem(j - g + count, count) == 1, last, first)
    tile = jnp.where(row < 4, jnp.sum(mass), jnp.max(speed))
    loc[...] = tile
    for j in range(count):
        out[j, 16] = tile


def pack_planes_kernel(ids, chip, rows, pair, red):
    b, g = ids[0], ids[1]
    core = lax.rem(b, 2)
    count = rows.shape[1]
    for t in range(4):
        src = lax.rem(g + t, count)
        for i in range(12):
            half = jnp.where(core == 0, i // 8, (4 + i) // 8)
            place = jnp.where(core == 0, i % 8, (4 + i) % 8)
            pair[4 * i + t] = rows[half, src, place]
    for f in range(4):
        for p in range(2):
            pair[48 + 2 * f + p] = chip[core, f + 1, 6 * core + p]
    mass, speed = rows[0, 0, 16], rows[0, 0, 16]
    for c in range(2):
        for j in range(count):
            if c + j > 0:
                mass = mass + rows[c, j, 16]
                speed = jnp.maximum(speed, rows[c, j, 16])
    lane = lax.broadcasted_iota(jnp.int32, (1, 128), 1)
    line = jnp.where(lane < 64, mass[0:1], speed[4:5])
    for j in range(red.shape[0]):
        red[j] = line


def fold_kernel(got, out):
    mass, speed = got[0], got[0]
    for j in range(1, got.shape[0]):
        mass = mass + got[j]
        speed = jnp.maximum(speed, got[j])
    lane = lax.broadcasted_iota(jnp.int32, (1, 128), 1)
    out[...] = jnp.broadcast_to(jnp.where(lane < 64, mass, speed), out.shape)


def plan_kernel(ids, boxes, plan):
    b = ids[0]
    core = lax.rem(b, 2)
    owner = jnp.clip(b + 2 * core - 1, 0, boxes.shape[0] // 2 - 1)
    second = jnp.logical_or(boxes[2 * owner] == 2 * b + 1, boxes[2 * owner + 1] == 2 * b + 1)
    plan[0] = jnp.where(second, 4, 0)
    for slot in range(2):
        plan[1 + slot] = boxes[2 * b + slot] - 2 * (b - core)


def main_kernel(ids, plan, loc, chip, rows, pairs, phi_out, delta, send,
                wide, fine, coarse_src, coarse_a, coarse_b, grav, prims, halo):
    b, g = ids[0], ids[1]
    core = lax.rem(b, 2)
    count = rows.shape[1]
    rho_loc = loc[0:1, :] * (1.0 / 8192.0)

    for t in range(4):
        own = lax.rem(g + t, count)
        at = pl.ds(8 * t, 8)
        for i in range(12):
            wide[i, at, :] = 2.0 * (rho_loc - pairs[0, 4 * i + t])
            wide[28 + i, at, :] = 2.0 * (rho_loc - pairs[1, 4 * i + t])
        for p in range(16):
            wide[12 + p, at, :] = 2.0 * (rho_loc - rows[p // 8, own, p % 8])
    src = wide.at[pl.ds(8 * core, 32)]

    def beside(below, here, above, step):
        total = below + above
        total = total + (roll(here, step, 0) + roll(here, -step, 0))
        return total + (roll(here, step, 1) + roll(here, -step, 1))

    head = 2.0 * W - 6.0 * W * W
    for p in range(1, 31):
        s = src[p]
        fine[p] = head * s + (W * W) * beside(src[p - 1], s, src[p + 1], 1)

    def residue(p):
        v = fine[p]
        return src[p] - 6.0 * v + beside(fine[p - 1], v, fine[p + 1], 1)

    even_y = lax.broadcasted_iota(jnp.int32, (32, 128), 0) % 2 == 0
    even_z = lax.broadcasted_iota(jnp.int32, (32, 128), 1) % 2 == 0
    for c in range(14):
        r = residue(2 + 2 * c) + residue(3 + 2 * c)
        r = r + jnp.where(even_y, roll(r, -1, 0), roll(r, 1, 0))
        r = r + jnp.where(even_z, roll(r, -1, 1), roll(r, 1, 1))
        coarse_src[c] = 0.5 * r
    for c in range(1, 13):
        s = coarse_src[c]
        coarse_a[c] = head * s + (W * W) * beside(coarse_src[c - 1], s, coarse_src[c + 1], 2)

    def relax(ref, right, n, step):
        v = ref[n]
        return (1.0 / 3.0) * v + W * (right + beside(ref[n - 1], v, ref[n + 1], step))

    for c in range(2, 12):
        coarse_b[c] = relax(coarse_a, coarse_src[c], c, 2)
    for c in range(3, 11):
        corr = relax(coarse_b, coarse_src[c], c, 2)
        for p in (2 * c + 2, 2 * c + 3):
            if 9 <= p <= 22:
                fine[p] = fine[p] + corr
    for p in range(10, 22):
        coarse_a[p - 9] = relax(fine, src[p], p, 1)
    for p in range(11, 21):
        coarse_b[p - 10] = relax(coarse_a, src[p], p - 9, 1)
    for p in range(8):
        v = coarse_b[p + 2]
        phi_out[p] = v[0:8]
        grav[0, p] = 0.5 * (coarse_b[p + 1, 0:8, :] - coarse_b[p + 3, 0:8, :])
        grav[1, p] = 0.5 * (roll(v, 1, 0) - roll(v, -1, 0))[0:8]
        own_rows = v[0:8]
        grav[2, p] = 0.5 * (roll(own_rows, 1, 1) - roll(own_rows, -1, 1))

    def put(ref, n, vals):
        for f, v in enumerate(prim_of(*vals)):
            ref[f, n] = v

    other = 1 - core
    for p in range(2):
        put(prims, 10 * core + p,
            [pairs[core, 40 * other + 4 * p]] + [pairs[core, 48 + 2 * f + p] for f in range(4)])
        put(prims, 10 * other + p, [chip[other, f, 6 * core + p] for f in range(5)])
    row = lax.broadcasted_iota(jnp.int32, (8, 128), 0)
    nxt = lax.rem(g + 1, count)
    prv = lax.rem(g + count - 1, count)
    for p in range(8):
        put(prims, 2 + p, [chip[core, f, p] for f in range(5)])
        ahead, behind = rows[core, nxt, 8 + p], rows[core, prv, 8 + p]
        vals = [jnp.where(row < 4, rows[core, nxt, p], rows[core, prv, p])]
        for k in range(4):
            vals.append(jnp.where(row < 4, roll(ahead, -2 * k, 0), roll(behind, 6 - 2 * k, 0)))
        put(halo, p, vals)

    def face_x(n):
        states = []
        for m, sign in ((n, 1.0), (n + 1, -1.0)):
            out = []
            for f in range(5):
                mid = prims[f, m]
                out.append(mid + sign * half_slope(mid - prims[f, m - 1], prims[f, m + 1] - mid))
            states.append(out)
        return hll(states[0], states[1], 0)

    def roll_faces(vals, normal, axis):
        left, right = [], []
        for v in vals:
            diff = roll(v, -1, axis) - v
            slope = half_slope(roll(diff, 1, axis), diff)
            left.append(v + slope)
            right.append(roll(v - slope, -1, axis))
        flux = hll(left, right, normal)
        return [fl - roll(fl, 1, axis) for fl in flux]

    def plane(p, before):
        after = face_x(p + 2)
        balance = [x - y for x, y in zip(after, before)]
        here = [prims[f, p + 2] for f in range(5)]
        tall = [jnp.concatenate([here[f], halo[f, p]], axis=0) for f in range(5)]
        for f, v in enumerate(roll_faces(tall, 1, 0)):
            balance[f] = balance[f] + v[0:8]
        for f, v in enumerate(roll_faces(here, 2, 1)):
            balance[f] = balance[f] + v
        pulls = [grav[d, p] for d in range(3)]
        moms = [chip[core, d + 1, p] for d in range(3)]
        delta[0, p] = -balance[0]
        for d in range(3):
            delta[d + 1, p] = chip[core, 0, p] * pulls[d] - balance[d + 1]
        delta[4, p] = (moms[0] * pulls[0] + moms[1] * pulls[1] + moms[2] * pulls[2]) - balance[4]
        return after

    face = face_x(1)
    for p in range(8):
        face = plane(p, face)

    start = plan[0]
    for f in range(5):
        for p in range(4):
            send[f, p] = chip[core, f, start + p]
            send[5 + f, p] = delta[f, start + p]


def final_kernel(plan, loc, got, chip, deltas, phi, came, out, potential, *, cells):
    mass = jnp.sum(got[...], axis=0, keepdims=True)
    speed = jnp.max(got[...], axis=0, keepdims=True)
    mass = jnp.broadcast_to(mass[:, 0:1], (1, 128))
    speed = jnp.broadcast_to(speed[:, 64:65], (1, 128))
    shift = CONST_GAIN * (mass / cells - loc[0:1, :] * (1.0 / 8192.0))
    step = COURANT / speed
    for p in range(8):
        potential[p] = phi[p] + shift
    for slot in range(2):
        place = plan[1 + slot]
        inside = jnp.logical_and(place >= 0, place <= 3)

        @pl.when(inside)
        def _():
            near = jnp.clip(place, 0, 3)
            half, start = near // 2, 4 * lax.rem(near, 2)
            for f in range(5):
                for p in range(4):
                    out[f, 4 * slot + p] = chip[half, f, start + p] + step * deltas[half, f, start + p]

        @pl.when(jnp.logical_not(inside))
        def _():
            for f in range(5):
                for p in range(4):
                    out[f, 4 * slot + p] = came[f, p] + step * came[5 + f, p]


def call(kernel, outs, ins, scratch, *args):
    spaces = {"s": pltpu.SMEM, "v": pltpu.VMEM, "h": pltpu.HBM}
    shapes, out_specs = [], []
    for shape in outs:
        scalar = len(shape) == 1
        shapes.append(jax.ShapeDtypeStruct(shape, jnp.int32 if scalar else F32))
        out_specs.append(pl.BlockSpec(memory_space=pltpu.SMEM if scalar else pltpu.VMEM))
    return pl.pallas_call(
        kernel,
        out_shape=shapes,
        in_specs=[pl.BlockSpec(memory_space=spaces[i]) for i in ins],
        out_specs=out_specs,
        scratch_shapes=scratch,
        compiler_params=pltpu.CompilerParams(vmem_limit_bytes=16 * 1024 * 1024),
    )(*args)


def shards(cs, boxes):
    ids = jnp.stack([lax.axis_index(BOX), lax.axis_index("x")]).astype(jnp.int32)
    n_box, n_grp = lax.axis_size(BOX), lax.axis_size("x")
    n_y, n_z = lax.axis_size("y"), lax.axis_size("z")
    cells = float(cs[0].size * n_box * n_grp)
    mates = [(i, (i + 2 * (i % 2) - 1) % n_box) for i in range(n_box)]

    packed, loc = call(pack_rows_kernel, [(n_grp, 17, 8, 128), (8, 128)], "sv", [], ids, cs)
    rows = lax.all_to_all(packed, "x", 0, 0, tiled=True)
    chip = lax.all_gather(cs, "c")
    boxes, chip = lax.optimization_barrier((boxes, chip))
    (plan,) = call(plan_kernel, [(3,)], "ss", [], ids, boxes)
    rows, plan = lax.optimization_barrier((rows, plan))
    rows = lax.all_gather(rows, "c")
    pair, red = call(pack_planes_kernel, [(56, 8, 128), (n_z, 1, 128)], "svv", [], ids, chip, rows)
    pair = lax.ppermute(pair, BOX, mates)
    red = lax.all_to_all(red, "z", 0, 0, tiled=True)
    pairs = lax.all_gather(pair, "c")
    state = (5, 8, 8, 128)
    sizes = [(40, 32, 128), (32, 32, 128), (14, 32, 128), (14, 32, 128), (14, 32, 128),
             (3, 8, 8, 128), (5, 12, 8, 128), state]
    phi, delta, send = call(
        main_kernel,
        [(8, 8, 128), state, (10, 4, 8, 128)],
        "ssvvvv",
        [pltpu.VMEM(size, F32) for size in sizes],
        ids, plan, loc, chip, rows, pairs)
    send, red = lax.optimization_barrier((send, red))
    (red,) = call(fold_kernel, [(n_y, 128)], "v", [], red)
    red = lax.all_to_all(red.reshape(n_y, 1, 128), "y", 0, 0, tiled=True)
    came = lax.ppermute(send, BOX, mates)
    deltas = lax.all_gather(delta, "c")

    def last(*refs):
        final_kernel(*refs, cells=cells)

    return call(last, [state, (8, 8, 128)], "svvvvvv", [],
                plan, loc, red.reshape(n_y, 128), chip, deltas, phi, came)


def solution(mesh):
    n_box, n_grp = mesh.devices.shape
    parts = (8, n_box // 16, 2) if n_box % 16 == 0 else (2, n_box // 4, 2)
    fine_mesh = Mesh(mesh.devices.reshape(*parts, n_grp), ("y", "z", "c", "x"))
    return jax.shard_map(
        lambda a, b: tuple(shards(a, b)),
        mesh=fine_mesh,
        in_specs=(P(None, BOX, "x", None), P()),
        out_specs=(P(None, BOX, "x", None), P(BOX, "x", None)),
        check_vma=False,
    )
```

```python
import jax
import jax.numpy as jnp
from jax import lax
from jax.experimental import pallas as pl
from jax.experimental.pallas import tpu as pltpu
from jax.sharding import Mesh, PartitionSpec as P

GAMMA = 5.0 / 3.0
COURANT = 0.3
W = (2.0 / 3.0) / 6.0
BOX = ("y", "z", "c")
F32 = jnp.float32
CONST_GAIN = 40.0 / 9.0


def roll(value, shift, axis):
    return pltpu.roll(value, shift % value.shape[axis], axis)


def prim_of(rho, mx, my, mz, energy):
    inv = 1.0 / rho
    vx, vy, vz = mx * inv, my * inv, mz * inv
    kinetic = 0.5 * (mx * vx + my * vy + mz * vz)
    return rho, vx, vy, vz, (GAMMA - 1.0) * (energy - kinetic)


def half_slope(back, ahead):
    low = jnp.minimum(back, ahead)
    high = jnp.maximum(back, ahead)
    return 0.5 * (jnp.maximum(low, 0.0) + jnp.minimum(high, 0.0))


def side(state, normal):
    rho, pressure = state[0], state[4]
    vel = state[1:4]
    u = vel[normal]
    mom = [rho * v for v in vel]
    energy = pressure * 1.5 + 0.5 * (mom[0] * vel[0] + mom[1] * vel[1] + mom[2] * vel[2])
    flux = [mom[normal]] + [mom[normal] * v for v in vel] + [u * (energy + pressure)]
    flux[1 + normal] = flux[1 + normal] + pressure
    sound = jnp.sqrt(GAMMA * pressure / rho)
    return [rho] + mom + [energy], flux, u - sound, u + sound


def hll(left, right, normal):
    cons_l, flux_l, slow_l, fast_l = side(left, normal)
    cons_r, flux_r, slow_r, fast_r = side(right, normal)
    low = jnp.minimum(jnp.minimum(slow_l, slow_r), 0.0)
    high = jnp.maximum(jnp.maximum(fast_l, fast_r), 0.0)
    inv = 1.0 / (high - low)
    a = high * inv
    b = low * inv
    ab = high * b
    return [a * fl - b * fr + ab * (cr - cl) for fl, fr, cl, cr in zip(flux_l, flux_r, cons_l, cons_r)]


def pack_rows_kernel(ids, cs, out, loc):
    g = ids[1]
    count = out.shape[0]
    row = lax.broadcasted_iota(jnp.int32, (8, 128), 0)
    mass = jnp.zeros((8, 128), F32)
    speed = jnp.zeros((8, 128), F32)
    for p in range(8):
        vals = [cs[f, p] for f in range(5)]
        rho, vx, vy, vz, pressure = prim_of(*vals)
        top = jnp.maximum(jnp.maximum(jnp.abs(vx), jnp.abs(vy)), jnp.abs(vz))
        speed = jnp.maximum(speed, top + jnp.sqrt(GAMMA * pressure / rho))
        mass = mass + rho
        last = jnp.zeros((8, 128), F32)
        first = jnp.zeros((8, 128), F32)
        for k in range(4):
            mine = (row // 2) == k
            last = jnp.where(mine, roll(vals[k + 1], 2 * k - 6, 0), last)
            first = jnp.where(mine, roll(vals[k + 1], 2 * k, 0), first)
        for j in range(count):
            out[j, p] = rho
            out[j, 8 + p] = jnp.where(lax.rem(j - g + count, count) == 1, last, first)
    tile = jnp.where(row < 4, jnp.sum(mass), jnp.max(speed))
    loc[...] = tile
    for j in range(count):
        out[j, 16] = tile


def pack_planes_kernel(ids, chip, rows, pair, red):
    b, g = ids[0], ids[1]
    core = lax.rem(b, 2)
    count = rows.shape[1]
    for t in range(4):
        src = lax.rem(g + t + count - 1, count)
        for i in range(12):
            half = jnp.where(core == 0, i // 8, (4 + i) // 8)
            place = jnp.where(core == 0, i % 8, (4 + i) % 8)
            pair[4 * i + t] = rows[half, src, place]
    for f in range(4):
        for p in range(2):
            pair[48 + 2 * f + p] = chip[core, f + 1, 6 * core + p]
    mass, speed = rows[0, 0, 16], rows[0, 0, 16]
    for c in range(2):
        for j in range(count):
            if c + j > 0:
                mass = mass + rows[c, j, 16]
                speed = jnp.maximum(speed, rows[c, j, 16])
    lane = lax.broadcasted_iota(jnp.int32, (1, 128), 1)
    line = jnp.where(lane < 64, mass[0:1], speed[4:5])
    for j in range(red.shape[0]):
        red[j] = jnp.broadcast_to(line, red.shape[1:])


def fold_kernel(got, out):
    mass, speed = got[0, 0:1], got[0, 0:1]
    for j in range(1, got.shape[0]):
        mass = mass + got[j, 0:1]
        speed = jnp.maximum(speed, got[j, 0:1])
    lane = lax.broadcasted_iota(jnp.int32, (1, 128), 1)
    out[...] = jnp.broadcast_to(jnp.where(lane < 64, mass, speed), out.shape)


def plan_kernel(ids, boxes, plan):
    b = ids[0]
    core = lax.rem(b, 2)
    owner = jnp.clip(b + 2 * core - 1, 0, boxes.shape[0] // 2 - 1)
    second = jnp.logical_or(boxes[2 * owner] == 2 * b + 1, boxes[2 * owner + 1] == 2 * b + 1)
    plan[0] = jnp.where(second, 4, 0)
    for slot in range(2):
        plan[1 + slot] = boxes[2 * b + slot] - 2 * (b - core)


def main_kernel(ids, plan, loc, chip, rows, pairs, phi_out, delta, send,
                wide, fine, spread, paired, coarse_src, coarse_a, coarse_b, post_a, post_b, grav, prims, halo):
    b, g = ids[0], ids[1]
    core = lax.rem(b, 2)
    count = rows.shape[1]
    rho_loc = loc[0:1, :] * (1.0 / 8192.0)

    for t in range(4):
        own = lax.rem(g + t + count - 1, count)
        at = pl.ds(8 * t, 8)
        for i in range(12):
            wide[i, at, :] = 2.0 * (rho_loc - pairs[0, 4 * i + t])
            wide[28 + i, at, :] = 2.0 * (rho_loc - pairs[1, 4 * i + t])
        for p in range(16):
            wide[12 + p, at, :] = 2.0 * (rho_loc - rows[p // 8, own, p % 8])
    src = wide.at[pl.ds(8 * core, 32)]

    def beside(below, here, above, step):
        total = below + above
        total = total + (roll(here, step, 0) + roll(here, -step, 0))
        return total + (roll(here, step, 1) + roll(here, -step, 1))

    head = 2.0 * W - 6.0 * W * W
    for p in range(1, 31):
        at = slice(0, 32) if 9 <= p <= 22 else slice(0, 24)
        s = src[p, at]
        fine[p, at] = head * s + (W * W) * beside(src[p - 1, at], s, src[p + 1, at], 1)

    even = lax.broadcasted_iota(jnp.int32, (16, 128), 1) % 2 == 0
    for c in range(14):
        low, high = 2 + 2 * c, 3 + 2 * c
        both = fine[low] + fine[high]
        near = (src[low] + src[high]) - 5.0 * both + (fine[low - 1] + fine[high + 1])
        evens, odds = pl.ds(32 * c, 16, stride=2), pl.ds(32 * c + 1, 16, stride=2)
        spread[32 * c:32 * c + 32, :] = near + (roll(both, 1, 0) + roll(both, -1, 0))
        paired[32 * c:32 * c + 32, :] = both
        r = spread[evens, :] + spread[odds, :]
        f = paired[evens, :] + paired[odds, :]
        r = r + (roll(f, 1, 1) + roll(f, -1, 1))
        coarse_src[c] = 0.5 * (r + jnp.where(even, roll(r, -1, 1), roll(r, 1, 1)))

    def beside_coarse(below, here, above):
        total = below + above
        total = total + (roll(here, 1, 0) + roll(here, -1, 0))
        return total + (roll(here, 2, 1) + roll(here, -2, 1))

    for c in range(1, 13):
        s = coarse_src[c]
        coarse_a[c] = head * s + (W * W) * beside_coarse(coarse_src[c - 1], s, coarse_src[c + 1])

    def relax_coarse(ref, c):
        v = ref[c]
        return (1.0 / 3.0) * v + W * (coarse_src[c] + beside_coarse(ref[c - 1], v, ref[c + 1]))

    for c in range(2, 12):
        coarse_b[c] = relax_coarse(coarse_a, c)
    for c in range(3, 11):
        corr = relax_coarse(coarse_b, c)
        spread[pl.ds(32 * c, 16, stride=2), :] = corr
        spread[pl.ds(32 * c + 1, 16, stride=2), :] = corr
        for p in (2 * c + 2, 2 * c + 3):
            if 9 <= p <= 22:
                fine[p, 0:24] = fine[p, 0:24] + spread[32 * c:32 * c + 24, :]

    def relax(below, v, above, right):
        return (1.0 / 3.0) * v + W * (right + beside(below, v, above, 1))

    for p in range(10, 22):
        post_a[p - 10] = relax(fine[p - 1, 0:24], fine[p, 0:24], fine[p + 1, 0:24], src[p, 0:24])
    for p in range(11, 21):
        post_b[p - 11] = relax(post_a[p - 11], post_a[p - 10], post_a[p - 9], src[p, 0:24])
    for p in range(8):
        v = post_b[p + 1]
        mine = v[8:16]
        phi_out[p] = mine
        grav[0, p] = 0.5 * (post_b[p, 8:16] - post_b[p + 2, 8:16])
        grav[1, p] = 0.5 * (roll(v, 1, 0) - roll(v, -1, 0))[8:16]
        grav[2, p] = 0.5 * (roll(mine, 1, 1) - roll(mine, -1, 1))

    def put(ref, n, vals):
        for f, v in enumerate(prim_of(*vals)):
            ref[f, n] = v

    other = 1 - core
    for p in range(2):
        put(prims, 10 * core + p,
            [pairs[core, 40 * other + 4 * p + 1]] + [pairs[core, 48 + 2 * f + p] for f in range(4)])
        put(prims, 10 * other + p, [chip[other, f, 6 * core + p] for f in range(5)])
    row = lax.broadcasted_iota(jnp.int32, (8, 128), 0)
    nxt = lax.rem(g + 1, count)
    prv = lax.rem(g + count - 1, count)
    for p in range(8):
        put(prims, 2 + p, [chip[core, f, p] for f in range(5)])
        ahead, behind = rows[core, nxt, 8 + p], rows[core, prv, 8 + p]
        vals = [jnp.where(row < 4, rows[core, nxt, p], rows[core, prv, p])]
        for k in range(4):
            vals.append(jnp.where(row < 4, roll(ahead, -2 * k, 0), roll(behind, 6 - 2 * k, 0)))
        put(halo, p, vals)

    def face_x(n):
        states = []
        for m, sign in ((n, 1.0), (n + 1, -1.0)):
            out = []
            for f in range(5):
                mid = prims[f, m]
                out.append(mid + sign * half_slope(mid - prims[f, m - 1], prims[f, m + 1] - mid))
            states.append(out)
        return hll(states[0], states[1], 0)

    def roll_faces(vals, normal, axis):
        left, right = [], []
        for v in vals:
            diff = roll(v, -1, axis) - v
            slope = half_slope(roll(diff, 1, axis), diff)
            left.append(v + slope)
            right.append(roll(v - slope, -1, axis))
        flux = hll(left, right, normal)
        return [fl - roll(fl, 1, axis) for fl in flux]

    def plane(p, before):
        after = face_x(p + 2)
        balance = [x - y for x, y in zip(after, before)]
        here = [prims[f, p + 2] for f in range(5)]
        tall = [jnp.concatenate([here[f], halo[f, p]], axis=0) for f in range(5)]
        for f, v in enumerate(roll_faces(tall, 1, 0)):
            balance[f] = balance[f] + v[0:8]
        for f, v in enumerate(roll_faces(here, 2, 1)):
            balance[f] = balance[f] + v
        pulls = [grav[d, p] for d in range(3)]
        moms = [chip[core, d + 1, p] for d in range(3)]
        delta[0, p] = -balance[0]
        for d in range(3):
            delta[d + 1, p] = chip[core, 0, p] * pulls[d] - balance[d + 1]
        delta[4, p] = (moms[0] * pulls[0] + moms[1] * pulls[1] + moms[2] * pulls[2]) - balance[4]
        return after

    face = face_x(1)
    for p in range(8):
        face = plane(p, face)

    start = plan[0]
    for f in range(5):
        for p in range(4):
            send[f, p] = chip[core, f, start + p]
            send[5 + f, p] = delta[f, start + p]


def final_kernel(plan, loc, got, chip, deltas, phi, came, out, potential, *, cells):
    mass = jnp.sum(got[...], axis=0, keepdims=True)
    speed = jnp.max(got[...], axis=0, keepdims=True)
    mass = jnp.broadcast_to(mass[:, 0:1], (1, 128))
    speed = jnp.broadcast_to(speed[:, 64:65], (1, 128))
    shift = CONST_GAIN * (mass / cells - loc[0:1, :] * (1.0 / 8192.0))
    step = COURANT / speed
    for p in range(8):
        potential[p] = phi[p] + shift
    for slot in range(2):
        place = plan[1 + slot]
        inside = jnp.logical_and(place >= 0, place <= 3)

        @pl.when(inside)
        def _():
            near = jnp.clip(place, 0, 3)
            half, start = near // 2, 4 * lax.rem(near, 2)
            for f in range(5):
                for p in range(4):
                    out[f, 4 * slot + p] = chip[half, f, start + p] + step * deltas[half, f, start + p]

        @pl.when(jnp.logical_not(inside))
        def _():
            for f in range(5):
                for p in range(4):
                    out[f, 4 * slot + p] = came[f, p] + step * came[5 + f, p]


def call(kernel, outs, ins, scratch, *args):
    spaces = {"s": pltpu.SMEM, "v": pltpu.VMEM, "h": pltpu.HBM}
    shapes, out_specs = [], []
    for shape in outs:
        scalar = len(shape) == 1
        shapes.append(jax.ShapeDtypeStruct(shape, jnp.int32 if scalar else F32))
        out_specs.append(pl.BlockSpec(memory_space=pltpu.SMEM if scalar else pltpu.VMEM))
    return pl.pallas_call(
        kernel,
        out_shape=shapes,
        in_specs=[pl.BlockSpec(memory_space=spaces[i]) for i in ins],
        out_specs=out_specs,
        scratch_shapes=scratch,
        compiler_params=pltpu.CompilerParams(vmem_limit_bytes=16 * 1024 * 1024),
    )(*args)


def shards(cs, boxes):
    ids = jnp.stack([lax.axis_index(BOX), lax.axis_index("x")]).astype(jnp.int32)
    n_box, n_grp = lax.axis_size(BOX), lax.axis_size("x")
    n_y, n_z = lax.axis_size("y"), lax.axis_size("z")
    cells = float(cs[0].size * n_box * n_grp)
    mates = [(i, (i + 2 * (i % 2) - 1) % n_box) for i in range(n_box)]

    packed, loc = call(pack_rows_kernel, [(n_grp, 17, 8, 128), (8, 128)], "sv", [], ids, cs)
    rows = lax.all_to_all(packed, "x", 0, 0, tiled=True)
    chip = lax.all_gather(cs, "c")
    boxes, chip = lax.optimization_barrier((boxes, chip))
    (plan,) = call(plan_kernel, [(3,)], "ss", [], ids, boxes)
    rows, plan = lax.optimization_barrier((rows, plan))
    rows = lax.all_gather(rows, "c")
    pair, red = call(pack_planes_kernel, [(56, 8, 128), (n_z, 8, 128)], "svv", [], ids, chip, rows)
    pair = lax.ppermute(pair, BOX, mates)
    red = lax.all_to_all(red, "z", 0, 0, tiled=True)
    pairs = lax.all_gather(pair, "c")
    state = (5, 8, 8, 128)
    sizes = [(40, 32, 128), (32, 32, 128), (448, 128), (448, 128), (14, 16, 128), (14, 16, 128), (14, 16, 128),
             (12, 24, 128), (10, 24, 128),
             (3, 8, 8, 128), (5, 12, 8, 128), state]
    phi, delta, send = call(
        main_kernel,
        [(8, 8, 128), state, (10, 4, 8, 128)],
        "ssvvvv",
        [pltpu.VMEM(size, F32) for size in sizes],
        ids, plan, loc, chip, rows, pairs)
    delta, red = lax.optimization_barrier((delta, red))
    (red,) = call(fold_kernel, [(n_y, 128)], "v", [], red)
    red = lax.all_to_all(red.reshape(n_y, 1, 128), "y", 0, 0, tiled=True)
    came = lax.ppermute(send, BOX, mates)
    deltas = lax.all_gather(delta, "c")

    def last(*refs):
        final_kernel(*refs, cells=cells)

    return call(last, [state, (8, 8, 128)], "svvvvvv", [],
                plan, loc, red.reshape(n_y, 128), chip, deltas, phi, came)


def solution(mesh):
    n_box, n_grp = mesh.devices.shape
    parts = (8, n_box // 16, 2) if n_box % 16 == 0 else (2, n_box // 4, 2)
    fine_mesh = Mesh(mesh.devices.reshape(*parts, n_grp), ("y", "z", "c", "x"))
    return jax.shard_map(
        lambda a, b: tuple(shards(a, b)),
        mesh=fine_mesh,
        in_specs=(P(None, BOX, "x", None), P()),
        out_specs=(P(None, BOX, "x", None), P(BOX, "x", None)),
        check_vma=False,
    )
```

```python
import jax
import jax.numpy as jnp
from jax import lax
from jax.experimental import pallas as pl
from jax.experimental.pallas import tpu as pltpu
from jax.sharding import Mesh, PartitionSpec as P

GAMMA = 5.0 / 3.0
COURANT = 0.3
W = (2.0 / 3.0) / 6.0
BOX = ("y", "z", "c")
F32 = jnp.float32
CONST_GAIN = 40.0 / 9.0


def roll(value, shift, axis):
    return pltpu.roll(value, shift % value.shape[axis], axis)


def prim_of(rho, mx, my, mz, energy):
    inv = 1.0 / rho
    vx, vy, vz = mx * inv, my * inv, mz * inv
    kinetic = 0.5 * (mx * vx + my * vy + mz * vz)
    return rho, vx, vy, vz, (GAMMA - 1.0) * (energy - kinetic)


def half_slope(back, ahead):
    low = jnp.minimum(back, ahead)
    high = jnp.maximum(back, ahead)
    return 0.5 * (jnp.maximum(low, 0.0) + jnp.minimum(high, 0.0))


def side(state, normal):
    rho, pressure = state[0], state[4]
    vel = state[1:4]
    u = vel[normal]
    mom = [rho * v for v in vel]
    energy = pressure * 1.5 + 0.5 * (mom[0] * vel[0] + mom[1] * vel[1] + mom[2] * vel[2])
    flux = [mom[normal]] + [mom[normal] * v for v in vel] + [u * (energy + pressure)]
    flux[1 + normal] = flux[1 + normal] + pressure
    sound = jnp.sqrt(GAMMA * pressure / rho)
    return [rho] + mom + [energy], flux, u - sound, u + sound


def hll(left, right, normal):
    cons_l, flux_l, slow_l, fast_l = side(left, normal)
    cons_r, flux_r, slow_r, fast_r = side(right, normal)
    low = jnp.minimum(jnp.minimum(slow_l, slow_r), 0.0)
    high = jnp.maximum(jnp.maximum(fast_l, fast_r), 0.0)
    inv = 1.0 / (high - low)
    a = high * inv
    b = low * inv
    ab = high * b
    return [a * fl - b * fr + ab * (cr - cl) for fl, fr, cl, cr in zip(flux_l, flux_r, cons_l, cons_r)]


def pack_rows_kernel(ids, cs, out, loc):
    g = ids[1]
    count = out.shape[0]
    row = lax.broadcasted_iota(jnp.int32, (8, 128), 0)
    mass = jnp.zeros((8, 128), F32)
    speed = jnp.zeros((8, 128), F32)
    for p in range(8):
        vals = [cs[f, p] for f in range(5)]
        rho, vx, vy, vz, pressure = prim_of(*vals)
        top = jnp.maximum(jnp.maximum(jnp.abs(vx), jnp.abs(vy)), jnp.abs(vz))
        speed = jnp.maximum(speed, top + jnp.sqrt(GAMMA * pressure / rho))
        mass = mass + rho
        last = jnp.zeros((8, 128), F32)
        first = jnp.zeros((8, 128), F32)
        for k in range(4):
            mine = (row // 2) == k
            last = jnp.where(mine, roll(vals[k + 1], 2 * k - 6, 0), last)
            first = jnp.where(mine, roll(vals[k + 1], 2 * k, 0), first)
        for j in range(count):
            out[j, p] = rho
            out[j, 8 + p] = jnp.where(lax.rem(j - g + count, count) == 1, last, first)
    tile = jnp.where(row < 4, jnp.sum(mass), jnp.max(speed))
    loc[...] = tile
    for j in range(count):
        out[j, 16] = tile


def pack_planes_kernel(ids, chip, rows, pair, red):
    b, g = ids[0], ids[1]
    core = lax.rem(b, 2)
    count = rows.shape[1]
    for t in range(4):
        src = lax.rem(g + t + count - 1, count)
        for i in range(12):
            half = jnp.where(core == 0, i // 8, (4 + i) // 8)
            place = jnp.where(core == 0, i % 8, (4 + i) % 8)
            pair[4 * i + t] = rows[half, src, place]
    for f in range(4):
        for p in range(2):
            pair[48 + 2 * f + p] = chip[core, f + 1, 6 * core + p]
    mass, speed = rows[0, 0, 16], rows[0, 0, 16]
    for c in range(2):
        for j in range(count):
            if c + j > 0:
                mass = mass + rows[c, j, 16]
                speed = jnp.maximum(speed, rows[c, j, 16])
    lane = lax.broadcasted_iota(jnp.int32, (1, 128), 1)
    line = jnp.where(lane < 64, mass[0:1], speed[4:5])
    for j in range(red.shape[0]):
        red[j] = jnp.broadcast_to(line, red.shape[1:])


def fold_kernel(got, out):
    mass, speed = got[0, 0:1], got[0, 0:1]
    for j in range(1, got.shape[0]):
        mass = mass + got[j, 0:1]
        speed = jnp.maximum(speed, got[j, 0:1])
    lane = lax.broadcasted_iota(jnp.int32, (1, 128), 1)
    out[...] = jnp.broadcast_to(jnp.where(lane < 64, mass, speed), out.shape)


def put(ref, n, vals):
    for f, v in enumerate(prim_of(*vals)):
        ref[f, n] = v


def face_x(prims, n):
    states = []
    for m, sign in ((n + 1, 1.0), (n + 2, -1.0)):
        out = []
        for f in range(5):
            mid = prims[f, m]
            out.append(mid + sign * half_slope(mid - prims[f, m - 1], prims[f, m + 1] - mid))
        states.append(out)
    return hll(states[0], states[1], 0)


def roll_faces(vals, normal, axis):
    left, right = [], []
    for v in vals:
        diff = roll(v, -1, axis) - v
        slope = half_slope(roll(diff, 1, axis), diff)
        left.append(v + slope)
        right.append(roll(v - slope, -1, axis))
    flux = hll(left, right, normal)
    return [fl - roll(fl, 1, axis) for fl in flux]


def plan_kernel(ids, boxes, chip, plan, inner, third, prims):
    b = ids[0]
    core = lax.rem(b, 2)
    owner = jnp.clip(b + 2 * core - 1, 0, boxes.shape[0] // 2 - 1)
    second = jnp.logical_or(boxes[2 * owner] == 2 * b + 1, boxes[2 * owner + 1] == 2 * b + 1)
    plan[0] = jnp.where(second, 4, 0)
    for slot in range(2):
        plan[1 + slot] = boxes[2 * b + slot] - 2 * (b - core)
    other = 1 - core
    for p in range(8):
        put(prims, 2 + p, [chip[core, f, p] for f in range(5)])
    for p in range(2):
        put(prims, 10 * other + p, [chip[other, f, 6 * core + p] for f in range(5)])
    for k in range(7):
        for f, v in enumerate(face_x(prims, 2 * other + k)):
            inner[f, 2 * other + k] = v
    for p in range(8):
        for f, v in enumerate(roll_faces([prims[f, p + 2] for f in range(5)], 2, 1)):
            third[f, p] = v


def main_kernel(ids, plan, loc, chip, rows, inner, third, pairs, phi_out, delta, send,
                wide, fine, spread, paired, coarse_src, coarse_a, coarse_b, post_a, post_b, grav, prims, halo):
    b, g = ids[0], ids[1]
    core = lax.rem(b, 2)
    count = rows.shape[1]
    rho_loc = loc[0:1, :] * (1.0 / 8192.0)

    for t in range(4):
        own = lax.rem(g + t + count - 1, count)
        at = pl.ds(8 * t, 8)
        for i in range(12):
            wide[i, at, :] = 2.0 * (rho_loc - pairs[0, 4 * i + t])
            wide[28 + i, at, :] = 2.0 * (rho_loc - pairs[1, 4 * i + t])
        for p in range(16):
            wide[12 + p, at, :] = 2.0 * (rho_loc - rows[p // 8, own, p % 8])
    src = wide.at[pl.ds(8 * core, 32)]

    def beside(below, here, above, step):
        total = below + above
        total = total + (roll(here, step, 0) + roll(here, -step, 0))
        return total + (roll(here, step, 1) + roll(here, -step, 1))

    head = 2.0 * W - 6.0 * W * W
    for p in range(1, 31):
        at = slice(0, 32) if 9 <= p <= 22 else slice(0, 24)
        s = src[p, at]
        fine[p, at] = head * s + (W * W) * beside(src[p - 1, at], s, src[p + 1, at], 1)

    even = lax.broadcasted_iota(jnp.int32, (16, 128), 1) % 2 == 0
    for c in range(14):
        low, high = 2 + 2 * c, 3 + 2 * c
        both = fine[low] + fine[high]
        near = (src[low] + src[high]) - 5.0 * both + (fine[low - 1] + fine[high + 1])
        evens, odds = pl.ds(32 * c, 16, stride=2), pl.ds(32 * c + 1, 16, stride=2)
        spread[32 * c:32 * c + 32, :] = near + (roll(both, 1, 0) + roll(both, -1, 0))
        paired[32 * c:32 * c + 32, :] = both
        r = spread[evens, :] + spread[odds, :]
        f = paired[evens, :] + paired[odds, :]
        r = r + (roll(f, 1, 1) + roll(f, -1, 1))
        coarse_src[c] = 0.5 * (r + jnp.where(even, roll(r, -1, 1), roll(r, 1, 1)))

    def beside_coarse(below, here, above):
        total = below + above
        total = total + (roll(here, 1, 0) + roll(here, -1, 0))
        return total + (roll(here, 2, 1) + roll(here, -2, 1))

    for c in range(1, 13):
        s = coarse_src[c]
        coarse_a[c] = head * s + (W * W) * beside_coarse(coarse_src[c - 1], s, coarse_src[c + 1])

    def relax_coarse(ref, c):
        v = ref[c]
        return (1.0 / 3.0) * v + W * (coarse_src[c] + beside_coarse(ref[c - 1], v, ref[c + 1]))

    for c in range(2, 12):
        coarse_b[c] = relax_coarse(coarse_a, c)
    for c in range(3, 11):
        corr = relax_coarse(coarse_b, c)
        spread[pl.ds(32 * c, 16, stride=2), :] = corr
        spread[pl.ds(32 * c + 1, 16, stride=2), :] = corr
        for p in (2 * c + 2, 2 * c + 3):
            if 9 <= p <= 22:
                fine[p, 0:24] = fine[p, 0:24] + spread[32 * c:32 * c + 24, :]

    def relax(below, v, above, right):
        return (1.0 / 3.0) * v + W * (right + beside(below, v, above, 1))

    for p in range(10, 22):
        post_a[p - 10] = relax(fine[p - 1, 0:24], fine[p, 0:24], fine[p + 1, 0:24], src[p, 0:24])
    for p in range(11, 21):
        post_b[p - 11] = relax(post_a[p - 11], post_a[p - 10], post_a[p - 9], src[p, 0:24])
    for p in range(8):
        v = post_b[p + 1]
        mine = v[8:16]
        phi_out[p] = mine
        grav[0, p] = 0.5 * (post_b[p, 8:16] - post_b[p + 2, 8:16])
        grav[1, p] = 0.5 * (roll(v, 1, 0) - roll(v, -1, 0))[8:16]
        grav[2, p] = 0.5 * (roll(mine, 1, 1) - roll(mine, -1, 1))

    other = 1 - core
    for p in range(2):
        put(prims, 10 * core + p,
            [pairs[core, 40 * other + 4 * p + 1]] + [pairs[core, 48 + 2 * f + p] for f in range(4)])
    row = lax.broadcasted_iota(jnp.int32, (8, 128), 0)
    nxt = lax.rem(g + 1, count)
    prv = lax.rem(g + count - 1, count)
    for p in range(8):
        put(prims, 2 + p, [chip[core, f, p] for f in range(5)])
        ahead, behind = rows[core, nxt, 8 + p], rows[core, prv, 8 + p]
        vals = [jnp.where(row < 4, rows[core, nxt, p], rows[core, prv, p])]
        for k in range(4):
            vals.append(jnp.where(row < 4, roll(ahead, -2 * k, 0), roll(behind, 6 - 2 * k, 0)))
        put(halo, p, vals)

    outer = [face_x(prims, 7 * core + k) for k in range(2)]

    def face(n):
        known = [inner[f, n] for f in range(5)]
        if n < 2:
            return [jnp.where(core == 0, o, k) for o, k in zip(outer[n], known)]
        if n > 6:
            return [jnp.where(core == 1, o, k) for o, k in zip(outer[n - 7], known)]
        return known

    def plane(p, before):
        after = face(p + 1)
        balance = [x - y + third[f, p] for f, (x, y) in enumerate(zip(after, before))]
        here = [prims[f, p + 2] for f in range(5)]
        tall = [jnp.concatenate([here[f], halo[f, p]], axis=0) for f in range(5)]
        for f, v in enumerate(roll_faces(tall, 1, 0)):
            balance[f] = balance[f] + v[0:8]
        pulls = [grav[d, p] for d in range(3)]
        moms = [chip[core, d + 1, p] for d in range(3)]
        delta[0, p] = -balance[0]
        for d in range(3):
            delta[d + 1, p] = chip[core, 0, p] * pulls[d] - balance[d + 1]
        delta[4, p] = (moms[0] * pulls[0] + moms[1] * pulls[1] + moms[2] * pulls[2]) - balance[4]
        return after

    edge = face(0)
    for p in range(8):
        edge = plane(p, edge)

    start = plan[0]
    for f in range(5):
        for p in range(4):
            send[f, p] = chip[core, f, start + p]
            send[5 + f, p] = delta[f, start + p]


def final_kernel(plan, loc, got, chip, deltas, phi, came, out, potential, *, cells):
    mass = jnp.sum(got[...], axis=0, keepdims=True)
    speed = jnp.max(got[...], axis=0, keepdims=True)
    mass = jnp.broadcast_to(mass[:, 0:1], (1, 128))
    speed = jnp.broadcast_to(speed[:, 64:65], (1, 128))
    shift = CONST_GAIN * (mass / cells - loc[0:1, :] * (1.0 / 8192.0))
    step = COURANT / speed
    for p in range(8):
        potential[p] = phi[p] + shift
    for slot in range(2):
        place = plan[1 + slot]
        inside = jnp.logical_and(place >= 0, place <= 3)

        @pl.when(inside)
        def _():
            near = jnp.clip(place, 0, 3)
            half, start = near // 2, 4 * lax.rem(near, 2)
            for f in range(5):
                for p in range(4):
                    out[f, 4 * slot + p] = chip[half, f, start + p] + step * deltas[half, f, start + p]

        @pl.when(jnp.logical_not(inside))
        def _():
            for f in range(5):
                for p in range(4):
                    out[f, 4 * slot + p] = came[f, p] + step * came[5 + f, p]


def call(kernel, outs, ins, scratch, *args):
    spaces = {"s": pltpu.SMEM, "v": pltpu.VMEM, "h": pltpu.HBM}
    shapes, out_specs = [], []
    for shape in outs:
        scalar = len(shape) == 1
        shapes.append(jax.ShapeDtypeStruct(shape, jnp.int32 if scalar else F32))
        out_specs.append(pl.BlockSpec(memory_space=pltpu.SMEM if scalar else pltpu.VMEM))
    return pl.pallas_call(
        kernel,
        out_shape=shapes,
        in_specs=[pl.BlockSpec(memory_space=spaces[i]) for i in ins],
        out_specs=out_specs,
        scratch_shapes=scratch,
        compiler_params=pltpu.CompilerParams(vmem_limit_bytes=16 * 1024 * 1024),
    )(*args)


def shards(cs, boxes):
    ids = jnp.stack([lax.axis_index(BOX), lax.axis_index("x")]).astype(jnp.int32)
    n_box, n_grp = lax.axis_size(BOX), lax.axis_size("x")
    n_y, n_z = lax.axis_size("y"), lax.axis_size("z")
    cells = float(cs[0].size * n_box * n_grp)
    mates = [(i, (i + 2 * (i % 2) - 1) % n_box) for i in range(n_box)]

    packed, loc = call(pack_rows_kernel, [(n_grp, 17, 8, 128), (8, 128)], "sv", [], ids, cs)
    rows = lax.all_to_all(packed, "x", 0, 0, tiled=True)
    chip = lax.all_gather(cs, "c")
    boxes, chip = lax.optimization_barrier((boxes, chip))
    plan, inner, third = call(
        plan_kernel, [(3,), (5, 9, 8, 128), (5, 8, 8, 128)], "ssv", [pltpu.VMEM((5, 12, 8, 128), F32)], ids, boxes, chip)
    rows, plan = lax.optimization_barrier((rows, plan))
    rows = lax.all_gather(rows, "c")
    pair, red = call(pack_planes_kernel, [(56, 8, 128), (n_z, 8, 128)], "svv", [], ids, chip, rows)
    pair = lax.ppermute(pair, BOX, mates)
    red = lax.all_to_all(red, "z", 0, 0, tiled=True)
    pairs = lax.all_gather(pair, "c")
    state = (5, 8, 8, 128)
    sizes = [(40, 32, 128), (32, 32, 128), (448, 128), (448, 128), (14, 16, 128), (14, 16, 128), (14, 16, 128),
             (12, 24, 128), (10, 24, 128),
             (3, 8, 8, 128), (5, 12, 8, 128), state]
    phi, delta, send = call(
        main_kernel,
        [(8, 8, 128), state, (10, 4, 8, 128)],
        "ssvvvvvv",
        [pltpu.VMEM(size, F32) for size in sizes],
        ids, plan, loc, chip, rows, inner, third, pairs)
    delta, red = lax.optimization_barrier((delta, red))
    (red,) = call(fold_kernel, [(n_y, 128)], "v", [], red)
    red = lax.all_to_all(red.reshape(n_y, 1, 128), "y", 0, 0, tiled=True)
    came = lax.ppermute(send, BOX, mates)
    deltas = lax.all_gather(delta, "c")

    def last(*refs):
        final_kernel(*refs, cells=cells)

    return call(last, [state, (8, 8, 128)], "svvvvvv", [],
                plan, loc, red.reshape(n_y, 128), chip, deltas, phi, came)


def solution(mesh):
    n_box, n_grp = mesh.devices.shape
    parts = (8, n_box // 16, 2) if n_box % 16 == 0 else (2, n_box // 4, 2)
    fine_mesh = Mesh(mesh.devices.reshape(*parts, n_grp), ("y", "z", "c", "x"))
    return jax.shard_map(
        lambda a, b: tuple(shards(a, b)),
        mesh=fine_mesh,
        in_specs=(P(None, BOX, "x", None), P()),
        out_specs=(P(None, BOX, "x", None), P(BOX, "x", None)),
        check_vma=False,
    )
```
